128 devices in a mesh: space: 16 (over z_hi, x, core), chan: 8 (over z_lo, y).
Axes of the slice: x: 4, y: 4, z: 4 (z_hi: 2, z_lo: 2; z = z_hi * 2 + z_lo), core: 2. Of those that a mesh axis runs over, the one named last changes fastest.
Arguments:
- activation: bfloat16 [96, 128, 1024], P('space', 'chan'), may hold values from -6 to 6
- cotangent: bfloat16 [96, 128, 1024], P('space', 'chan'), may hold values from -6 to 6
- kernel: bfloat16 [3, 3, 3, 128, 128], P(None, None, None, None, 'chan'), may hold values from -0.109375 to 0.109375
Outputs:
- output: bfloat16 [96, 128, 1024], P('space', 'chan')
- grad_input: bfloat16 [96, 128, 1024], P('space', 'chan')
- grad_kernel: float32 [3, 3, 3, 128, 128], P(None, None, None, None, 'chan')
The draws below stay inside these ranges and needn't reach their ends.
All inputs are finite; a program needn't handle non-finite values.
Results may differ from the reference program's by a relative error of at most 0.0029.
Values may be sent and summed in bfloat16 or wider, within the bound.
No kernel may reach another device: no remote copies, remote signals or barrier semaphores. Data moves between devices by JAX's collectives and lax.ppermute only.
A program may use at most 64 MiB of HBM per device.

```python
import math
import jax
import jax.numpy as jnp
from jax import lax

C = 128
NXY = 32
NZ = 96


def level_of(stream_key, extent, pieces, least, top_value):
    def one(dim, blocks):
        steps = jax.random.uniform(jax.random.fold_in(jax.random.fold_in(stream_key, 6), dim), (blocks,), jnp.float32, least / len(pieces), top_value / len(pieces))
        return jnp.repeat(jnp.exp(steps), extent[dim] // blocks).reshape((-1,) + (1,) * (len(extent) - dim - 1))

    loudness = one(*pieces[0])
    for cut in pieces[1:]:
        loudness = loudness * one(*cut)
    return loudness


def centred(rng, extent, width, most, split=(), kind=jnp.bfloat16):
    values = jax.random.normal(rng, extent, jnp.float32) * width
    if len(split) > 0:
        values = level_of(rng, extent, split, -0.22, 0.18) * values
    return jnp.clip(values, min=-most, max=most).astype(kind)


def setup_inputs(seed: int = 0) -> dict:
    key_list = jax.random.split(jax.random.key(seed), 4)
    return {
        "activation": centred(key_list[0], (NZ, C, NXY * NXY), 1.0, 6.0, ((0, 16), (1, 8))),
        "cotangent": centred(key_list[1], (NZ, C, NXY * NXY), 1.0, 6.0, ((0, 16), (1, 8))),
        "kernel": centred(key_list[2], (3, 3, 3, C, C), (27 * C) ** -0.5, 0.109375, ((4, 8),)),
    }


def periodic_conv(field, filt):
    padded = jnp.pad(field, ((1, 1), (0, 0), (1, 1), (1, 1)), mode='wrap')
    result = lax.conv_general_dilated(padded[None], filt, (1, 1, 1), 'VALID', dimension_numbers=('NDCHW', 'DHWIO', 'NDCHW'), preferred_element_type=jnp.float32)
    return result[0]

def reference(activation, cotangent, kernel):
    depth, chans, cells = (activation.shape[0], activation.shape[1], activation.shape[2])
    side = NXY
    act4 = activation.reshape(depth, chans, side, side)
    cot4 = cotangent.reshape(depth, chans, side, side)
    output = periodic_conv(act4, kernel).astype(jnp.bfloat16).reshape(depth, chans, cells)
    flipped = jnp.swapaxes(jnp.flip(kernel, (0, 1, 2)), 3, 4)
    grad_input = periodic_conv(cot4, flipped).astype(jnp.bfloat16).reshape(depth, chans, cells)
    padded = jnp.pad(act4, ((1, 1), (0, 0), (1, 1), (1, 1)), mode='wrap').astype(jnp.float32)
    cot_wide = cot4.astype(jnp.float32)
    taps = []
    for a in range(3):
        for b in range(3):
            for c in range(3):
                window = padded[a:a + depth, :, b:b + side, c:c + side]
                taps.append(jnp.einsum('zixy,zoxy->io', window, cot_wide))
    factor = 1.0 / math.sqrt(float(depth * side * side))
    grad_kernel = jnp.stack(taps).reshape(3, 3, 3, chans, chans) * factor
    return (output, grad_input, grad_kernel)
```

```python
import functools

import jax
import jax.numpy as jnp
from jax import lax
from jax.experimental import pallas as pl
from jax.experimental.pallas import tpu as pltpu
from jax.sharding import Mesh, PartitionSpec as P

NXY = 32
CELLS = NXY * NXY
C = 128
PLANES = 6
SPACE = ("zh", "x", "core")
CHAN = ("zl", "y")
BF = jnp.bfloat16
F32 = jnp.float32
VMEM_LIMIT = 56 * 1024 * 1024


def perm(v, axis, k):
    n = lax.axis_size(axis)
    return lax.ppermute(v, axis, [(i, (i + k) % n) for i in range(n)])


def outer_swap(v):
    n = 16
    pairs = []
    for i in range(1, n, 2):
        j = (i + 1) % n
        pairs += [(i, j), (j, i)]
    return lax.ppermute(v, SPACE, pairs)


def gather_units(u):
    z1 = perm(u, "zl", 1)
    a = perm(u, "y", 1)
    b = perm(u, "y", -1)
    c = perm(a, "y", 1)
    d = perm(z1, "y", -1)
    e = perm(a, "zl", 1)
    f = perm(c, "zl", 1)
    return {(0, 0): u, (1, 0): z1, (0, 3): a, (0, 1): b, (0, 2): c, (1, 1): d, (1, 3): e, (1, 2): f}


KEYS = [(0, 0), (0, 1), (0, 2), (0, 3), (1, 0), (1, 1), (1, 2), (1, 3)]


def lane_y(rows):
    return lax.broadcasted_iota(jnp.int32, (rows, CELLS), 1) % NXY


def from_y_before(v, y):
    return jnp.where(y == 0, pltpu.roll(v, CELLS - (NXY - 1), 1), pltpu.roll(v, 1, 1))


def from_y_after(v, y):
    return jnp.where(y == NXY - 1, pltpu.roll(v, NXY - 1, 1), pltpu.roll(v, CELLS - 1, 1))


def own_row(key):
    zl = lax.axis_index("zl")
    y = lax.axis_index("y")
    group = lax.rem(zl + key[0], 2) * 4 + lax.rem(y + key[1], 4)
    return pl.multiple_of(group * 16, 16)


def gk_body(*refs):
    units, (g, gb, ga), (keep, send), (field, g9, acc) = refs[:8], refs[8:11], refs[11:13], refs[13:]
    for key, unit in zip(KEYS, units):
        row = own_row(key)
        for z in range(PLANES):
            field[z, pl.ds(row, 16), :] = unit[z]
    y = lane_y(16)
    for p in range(PLANES + 2):
        plane = (gb[0] if p == 0 else ga[0] if p == PLANES + 1 else g[p - 1]).astype(F32)
        slot = PLANES + 1 - p
        for c, v in enumerate((from_y_after(plane, y), plane, from_y_before(plane, y))):
            for b, w in enumerate((pltpu.roll(v, CELLS - NXY, 1), v, pltpu.roll(v, NXY, 1))):
                g9[pl.ds(slot * 144 + (b * 3 + c) * 16, 16), :] = w.astype(BF)
    total = None
    for z in range(PLANES):
        lhs = g9[pl.ds((PLANES - 1 - z) * 144, 432), :]
        term = lax.dot_general(lhs, field[z], (((1,), (1,)), ((), ())), preferred_element_type=F32)
        total = term if total is None else total + term
    acc[...] = total
    core = lax.axis_index("core")
    keep[...] = acc[pl.ds(pl.multiple_of(core * 216, 8), 216), :]
    send[...] = acc[pl.ds(pl.multiple_of((1 - core) * 216, 8), 216), :]


def conv_body(absolute, *refs):
    units, w, (mid, edge, away), (field,) = refs[:8], refs[8], refs[9:12], refs[12:]
    for n, (key, unit) in enumerate(zip(KEYS, units)):
        row = own_row(key) if absolute else n * 16
        for z in range(PLANES):
            field[z, pl.ds(row, 16), :] = unit[z]
    y = lane_y(16)
    for z in range(-1, PLANES + 1):
        taps = [a for a in range(3) if 0 <= z + a - 1 < PLANES]
        lhs = jnp.concatenate([w[pl.ds(a * 144, 144), :] for a in taps], axis=1)
        first = z + taps[0] - 1
        rhs = field[pl.ds(first, len(taps))].reshape(len(taps) * C, CELLS)
        t = jnp.dot(lhs, rhs, preferred_element_type=F32)
        s = t[48:96] + pltpu.roll(t[0:48], NXY, 1) + pltpu.roll(t[96:144], CELLS - NXY, 1)
        out = s[16:32] + from_y_before(s[0:16], y) + from_y_after(s[32:48], y)
        if z == -1:
            away[0] = out
        elif z == PLANES:
            away[1] = out
        elif z == 0:
            edge[0] = out
        elif z == PLANES - 1:
            edge[1] = out
        else:
            mid[z - 1] = out.astype(BF)


def cost(flops, size):
    return pl.CostEstimate(flops=flops, bytes_accessed=size, transcendentals=0)


def gk_call(units, g, gb, ga):
    vm = pl.BlockSpec(memory_space=pltpu.VMEM)
    return pl.pallas_call(
        gk_body,
        out_shape=[jax.ShapeDtypeStruct((216, C), F32)] * 2,
        in_specs=[vm] * 11,
        out_specs=[vm] * 2,
        scratch_shapes=[
            pltpu.VMEM((PLANES, C, CELLS), BF),
            pltpu.VMEM(((PLANES + 2) * 144, CELLS), BF),
            pltpu.VMEM((432, C), F32),
        ],
        compiler_params=pltpu.CompilerParams(vmem_limit_bytes=VMEM_LIMIT),
        cost_estimate=cost(2 * 432 * C * CELLS * PLANES, 4 << 20),
        name="grad_kernel_terms",
    )(*[units[k] for k in KEYS], g, gb, ga)


def conv_call(units, w, absolute, name):
    vm = pl.BlockSpec(memory_space=pltpu.VMEM)
    return pl.pallas_call(
        functools.partial(conv_body, absolute),
        out_shape=[
            jax.ShapeDtypeStruct((PLANES - 2, 16, CELLS), BF),
            jax.ShapeDtypeStruct((2, 16, CELLS), F32),
            jax.ShapeDtypeStruct((2, 16, CELLS), F32),
        ],
        in_specs=[vm] * 9,
        out_specs=[vm] * 3,
        scratch_shapes=[pltpu.VMEM((PLANES, C, CELLS), BF)],
        compiler_params=pltpu.CompilerParams(vmem_limit_bytes=VMEM_LIMIT),
        cost_estimate=cost(2 * 432 * C * CELLS * PLANES, 4 << 20),
        name=name,
    )(*[units[k] for k in KEYS], w)


def swap_edges(away, core):
    inner = lax.ppermute(jnp.where(core == 0, away[1], away[0]), "core", [(0, 1), (1, 0)])
    outer = outer_swap(jnp.where(core == 0, away[0], away[1]))
    return jnp.where(core == 0, outer, inner), jnp.where(core == 0, inner, outer)


def finish(mid, edge, away, core):
    low, high = swap_edges(away, core)
    first = (edge[0] + low).astype(BF)[None]
    last = (edge[1] + high).astype(BF)[None]
    return jnp.concatenate([first, mid, last], axis=0)


def exchange_filter(kt, zl, y):
    parts = kt.reshape(27, 16, 8, 16).transpose(2, 0, 1, 3).reshape(8, 54, 128)
    theirs = lax.dynamic_slice_in_dim(parts, (1 - zl) * 4, 4, 0)
    mine = lax.dynamic_slice_in_dim(parts, zl * 4, 4, 0)
    both = jnp.stack([mine, perm(theirs, "zl", 1)], axis=1)
    got = {}
    for k in range(4):
        part = lax.dynamic_index_in_dim(both, (y + k) % 4, 0, keepdims=False)
        part = part if k == 0 else perm(part, "y", k)
        for r in range(2):
            got[(r, (4 - k) % 4)] = part[r]
    full = jnp.stack([got[k] for k in KEYS]).reshape(8, 27, 16, 16)
    return full[:, ::-1].transpose(1, 3, 0, 2).reshape(432, 128)


def sum_over_space(keep, send, core):
    half = keep + lax.ppermute(send, "core", [(0, 1), (1, 0)])
    across = half + perm(half, "x", 2)
    sides = perm(half, "x", 1) + perm(half, "x", -1)
    row = across + sides
    total = row + perm(row, "zh", 1)
    other = lax.ppermute(total, "core", [(0, 1), (1, 0)])
    low = jnp.where(core == 0, total, other)
    high = jnp.where(core == 0, other, total)
    return jnp.concatenate([low, high], axis=0)


def on_device(activation, cotangent, kernel):
    core, zl, y = lax.axis_index("core"), lax.axis_index("zl"), lax.axis_index("y")
    kt = jnp.swapaxes(kernel, 3, 4).reshape(27, 16, 128)
    a_units = gather_units(activation)
    g_inner = lax.ppermute(jnp.where(core == 0, cotangent[5], cotangent[0])[None], "core", [(0, 1), (1, 0)])
    g_outer = outer_swap(jnp.where(core == 0, cotangent[0], cotangent[5])[None])
    gb = jnp.where(core == 0, g_outer, g_inner)
    ga = jnp.where(core == 0, g_inner, g_outer)
    keep, send = gk_call(a_units, cotangent, gb, ga)
    w_in = exchange_filter(kt, zl, y)
    g_units = gather_units(cotangent)
    output = finish(*conv_call(a_units, kt.reshape(432, 128), True, "output_planes"), core)
    grad_input = finish(*conv_call(g_units, w_in, False, "grad_input_planes"), core)
    scale = 98304.0**-0.5
    total = sum_over_space(keep, send, core) * scale
    grad_kernel = jnp.swapaxes(total.reshape(3, 3, 3, 16, 128), 3, 4)
    return (output, grad_input, grad_kernel)


def solution(mesh):
    fine = Mesh(mesh.devices.reshape(2, 4, 2, 2, 4), SPACE + CHAN)
    field = P(SPACE, CHAN, None)
    filt = P(None, None, None, None, CHAN)
    return jax.shard_map(
        on_device,
        mesh=fine,
        in_specs=(field, field, filt),
        out_specs=(field, field, filt),
        check_vma=False,
    )
```

```python
import functools

import jax
import jax.numpy as jnp
from jax import lax
from jax.experimental import pallas as pl
from jax.experimental.pallas import tpu as pltpu
from jax.sharding import Mesh, PartitionSpec as P

NXY = 32
CELLS = NXY * NXY
C = 128
N = 6
SPACE = ("zh", "x", "core")
CHAN = ("zl", "y")
BF = jnp.bfloat16
F32 = jnp.float32
VMEM_LIMIT = 56 * 1024 * 1024
VM = pl.BlockSpec(memory_space=pltpu.VMEM)
KEYS = [(0, 0), (0, 1), (0, 2), (0, 3), (1, 0), (1, 1), (1, 2), (1, 3)]


def swap(v, axis, bits):
    return lax.ppermute(v, axis, [(i, i ^ bits) for i in range(lax.axis_size(axis))])


def outer_swap(v):
    pairs = []
    for i in range(1, 16, 2):
        j = (i + 1) % 16
        pairs += [(i, j), (j, i)]
    return lax.ppermute(v, SPACE, pairs)


def after(v, *deps):
    return lax.optimization_barrier((v,) + deps)[0]


def group(key):
    return (lax.axis_index("zl") ^ key[0]) * 4 + (lax.axis_index("y") ^ key[1])


def first_row(key):
    return pl.multiple_of(group(key) * 16, 16)


def lane_y():
    return lax.broadcasted_iota(jnp.int32, (16, CELLS), 1) % NXY


def from_y_before(v, y):
    return jnp.where(y == 0, pltpu.roll(v, CELLS - (NXY - 1), 1), pltpu.roll(v, 1, 1))


def from_y_after(v, y):
    return jnp.where(y == NXY - 1, pltpu.roll(v, NXY - 1, 1), pltpu.roll(v, CELLS - 1, 1))


def assemble(blocks, field, absolute, pair):
    for n, (key, (ref, start)) in enumerate(zip(KEYS, blocks)):
        row = first_row(key) if absolute else n * 16
        for z in (2 * pair, 2 * pair + 1):
            field[z, pl.ds(row, 16), :] = ref[start + z]


def pack_filter_body(k_ref, near, far, turned):
    turned[:, 0:432] = jnp.transpose(k_ref[...].astype(F32))
    turned[:, 432:512] = jnp.zeros((C, 80), F32)
    for ry in range(4):
        near[pl.ds(ry * 16, 16), :] = turned[pl.ds(first_row((0, ry)), 16), :].astype(BF)
        far[pl.ds(ry * 16, 16), :] = turned[pl.ds(first_row((1, ry)), 16), :].astype(BF)


def unpack_filter_body(near, far, got1, got3, w_ref):
    lane = lax.broadcasted_iota(jnp.int32, (16, C), 1) // 16
    pieces = {
        (0, 0): near[0:16],
        (1, 0): far[0:16],
        (0, 1): got1[0:16],
        (1, 1): got1[32:48],
        (0, 2): got3[0:16],
        (0, 3): got3[16:32],
        (1, 2): got3[32:48],
        (1, 3): got3[48:64],
    }
    pieces = {k: v.astype(F32) for k, v in pieces.items()}
    for tap in range(27):
        tile, spot = divmod(tap * 16, C)
        row = jnp.zeros((16, C), F32)
        for n, key in enumerate(KEYS):
            v = pieces[key][:, tile * C : (tile + 1) * C]
            move = (n * 16 - spot) % C
            v = v if move == 0 else pltpu.roll(v, move, 1)
            row = jnp.where(lane == n, v, row)
        w_ref[pl.ds((26 - tap) * 16, 16), :] = row.astype(BF)


def gk_body(*refs):
    units, (g, g_in, g_out), (out,), (field, g9) = refs[:8], refs[8:11], refs[11:12], refs[12:]
    core = lax.axis_index("core")
    y = lane_y()
    for p in range(N + 2):
        if p == 0:
            plane = jnp.where(core == 0, g_out[0].astype(F32), g_in[0].astype(F32))
        elif p == N + 1:
            plane = jnp.where(core == 0, g_in[0].astype(F32), g_out[0].astype(F32))
        else:
            plane = g[p - 1].astype(F32)
        slot = N + 1 - p
        for c, v in enumerate((from_y_after(plane, y), plane, from_y_before(plane, y))):
            for b, w in enumerate((pltpu.roll(v, CELLS - NXY, 1), v, pltpu.roll(v, NXY, 1))):
                g9[pl.ds(slot * 144 + (b * 3 + c) * 16, 16), :] = w.astype(BF)
    for pair in range(N // 2):
        assemble([(u, 0) for u in units], field, True, pair)
        z = 2 * pair
        lhs = g9[pl.ds((N - 2 - z) * 144, 576), :]
        rhs = field[pl.ds(z, 2)].reshape(2 * C, CELLS)
        term = lax.dot_general(lhs, rhs, (((1,), (1,)), ((), ())), preferred_element_type=F32)
        term = term[144:576, 0:C] + term[0:432, C : 2 * C]
        if pair == 0:
            out[...] = term
        else:
            out[...] += term


def conv_planes(blocks, absolute, field, w, carry, out_ref, edge):
    y = lane_y()
    w0, w1, w2 = (w[pl.ds(a * 144, 144), :] for a in range(3))
    none = jnp.zeros((144, C), BF)
    lhs = jnp.concatenate(
        [jnp.concatenate(row, axis=1) for row in ((w2, none), (w1, w2), (w0, w1), (none, w0))], axis=0
    )
    beyond = []
    for pair in range(N // 2):
        assemble(blocks, field, absolute, pair)
        rhs = field[pl.ds(2 * pair, 2)].reshape(2 * C, CELLS)
        terms = jnp.dot(lhs, rhs, preferred_element_type=F32)
        last = pair == N // 2 - 1
        for n in range(4):
            z = 2 * pair - 1 + n
            t = terms[n * 144 : n * 144 + 144]
            if n < 2 and pair > 0:
                t = t + carry[pl.ds(n * 144, 144), :]
            if n >= 2 and not last:
                carry[pl.ds((n - 2) * 144, 144), :] = t
                continue
            s = t[48:96] + pltpu.roll(t[0:48], NXY, 1) + pltpu.roll(t[96:144], CELLS - NXY, 1)
            out = s[16:32] + from_y_before(s[0:16], y) + from_y_after(s[32:48], y)
            if z in (-1, N):
                beyond.append(out)
            elif z in (0, N - 1):
                edge[0 if z == 0 else 1] = out
            else:
                out_ref[z] = out.astype(BF)
    out_ref[0] = jnp.zeros((16, CELLS), BF)
    out_ref[N - 1] = jnp.zeros((16, CELLS), BF)
    return beyond


def output_body(*refs):
    units, w, (out_ref, edge, inner, outer), (field, carry) = refs[:8], refs[8], refs[9:13], refs[13:]
    before, behind = conv_planes([(u, 0) for u in units], True, field, w, carry, out_ref, edge)
    first = lax.axis_index("core") == 0
    inner[...] = jnp.where(first, behind, before)
    outer[...] = jnp.where(first, before, behind)


def grad_input_body(*refs):
    units, (w, inner0, outer0), (out_ref, edge, inner, outer), (field, carry) = refs[:8], refs[8:11], refs[11:15], refs[15:]
    starts = [0 if key in ((0, 0), (1, 2)) else N for key in KEYS]
    inner[0] = inner0[...]
    outer[0] = outer0[...]
    before, behind = conv_planes(list(zip(units, starts)), False, field, w, carry, out_ref, edge)
    first = lax.axis_index("core") == 0
    inner[1] = jnp.where(first, behind, before)
    outer[1] = jnp.where(first, before, behind)


def finish_body(o_in, o_edge, g_in, g_edge, inner, outer, o_ref, g_ref):
    first = lax.axis_index("core") == 0
    for n, (src, edge, dst) in enumerate(((o_in, o_edge, o_ref), (g_in, g_edge, g_ref))):
        dst[pl.ds(1, N - 2)] = src[pl.ds(1, N - 2)]
        low = jnp.where(first, outer[n], inner[n])
        high = jnp.where(first, inner[n], outer[n])
        dst[0] = (edge[0] + low).astype(BF)
        dst[N - 1] = (edge[1] + high).astype(BF)


def call(body, name, args, specs, outs, scratch=(), flops=0, size=1 << 20):
    return pl.pallas_call(
        body,
        out_shape=[jax.ShapeDtypeStruct(s, d) for s, d in outs],
        in_specs=specs,
        out_specs=[VM] * len(outs),
        scratch_shapes=list(scratch),
        compiler_params=pltpu.CompilerParams(vmem_limit_bytes=VMEM_LIMIT),
        cost_estimate=pl.CostEstimate(flops=flops, bytes_accessed=size, transcendentals=0),
        name=name,
    )(*args)


CONV_FLOPS = 2 * 432 * C * CELLS * N
FIELD = [pltpu.VMEM((N, C, CELLS), BF)]


def on_device(activation, cotangent, kernel):
    core = lax.axis_index("core")
    kt = jnp.swapaxes(kernel, 3, 4).reshape(432, C)

    own = jnp.concatenate([activation, cotangent], axis=0)
    k1 = swap(own, "y", 1)
    z0 = swap(own, "zl", 1)
    k3 = swap(own, "y", 3)
    g_in = swap(jnp.where(core == 0, cotangent[N - 1 :], cotangent[:1]), "core", 1)
    g_out = outer_swap(jnp.where(core == 0, cotangent[:1], cotangent[N - 1 :]))
    k2 = swap(k1, "y", 3)
    z1 = swap(z0, "y", 1)
    z3 = swap(k3, "zl", 1)
    z2a = swap(k2[:N], "zl", 1)
    z2g = swap(z3[N:], "y", 1)

    near, far = call(
        pack_filter_body, "pack_filter", [kt], [VM], [((64, 512), BF)] * 2, [pltpu.VMEM((C, 512), F32)]
    )
    far = swap(after(far, k1, z0, k3, g_out), "zl", 1)
    got1 = swap(jnp.concatenate([near[16:48], far[16:48]]), "y", 1)
    got3 = swap(after(jnp.concatenate([got1[16:32], near[48:64], got1[48:64], far[48:64]]), k2), "y", 3)
    w_in = call(
        unpack_filter_body,
        "unpack_filter",
        [near, far, got1, got3],
        [VM] * 4,
        [((432, C), BF)],
    )[0]

    activation = after(activation, got3)
    a_units = [activation, k1, k2, k3, z0, z1, z2a, z3]
    g_units = [cotangent, k1, k2, k3, z0, z1, z2g, z3]
    terms = call(
        gk_body,
        "grad_kernel_terms",
        [*a_units, cotangent, g_in, g_out],
        [VM] * 8 + [VM] * 3,
        [((432, C), F32)],
        FIELD + [pltpu.VMEM(((N + 2) * 144, CELLS), BF)],
        CONV_FLOPS,
        4 << 20,
    )[0]
    terms = terms + swap(terms, "core", 1)
    got = swap(terms, "x", 1)

    conv_outs = [((N, 16, CELLS), BF), ((2, 16, CELLS), F32)]
    conv_scratch = FIELD + [pltpu.VMEM((288, CELLS), F32)]
    a_units[0] = after(activation, terms)
    out0, edge0, inner0, outer0 = call(
        output_body,
        "output_planes",
        [*a_units, kt],
        [VM] * 8 + [VM],
        conv_outs + [((16, CELLS), F32)] * 2,
        conv_scratch,
        CONV_FLOPS,
        4 << 20,
    )
    terms = after(terms, edge0, w_in) + got
    got = swap(terms, "x", 3)
    g_units[0] = after(cotangent, terms)
    out1, edge1, inner, outer = call(
        grad_input_body,
        "grad_input_planes",
        [*g_units, w_in, inner0, outer0],
        [VM] * 8 + [VM] * 3,
        conv_outs + [((2, 16, CELLS), F32)] * 2,
        conv_scratch,
        CONV_FLOPS,
        4 << 20,
    )
    outer = outer_swap(outer)
    inner = swap(inner, "core", 1)
    terms = (after(terms, edge1) + got).astype(BF)
    terms = terms.astype(F32) + swap(terms, "zh", 1).astype(F32)
    output, grad_input = call(
        finish_body,
        "finish_planes",
        [out0, edge0, out1, edge1, inner, outer],
        [VM] * 6,
        [((N, 16, CELLS), BF)] * 2,
    )
    grad_kernel = jnp.swapaxes((terms * 98304.0**-0.5).reshape(3, 3, 3, 16, C), 3, 4)
    return (output, grad_input, grad_kernel)


def solution(mesh):
    fine = Mesh(mesh.devices.reshape(2, 4, 2, 2, 4), SPACE + CHAN)
    field = P(SPACE, CHAN, None)
    filt = P(None, None, None, None, CHAN)
    return jax.shard_map(
        on_device,
        mesh=fine,
        in_specs=(field, field, filt),
        out_specs=(field, field, filt),
        check_vma=False,
    )
```

```python
import functools

import jax
import jax.numpy as jnp
from jax import lax
from jax.experimental import pallas as pl
from jax.experimental.pallas import tpu as pltpu
from jax.sharding import Mesh, PartitionSpec as P

NXY = 32
CELLS = NXY * NXY
C = 128
N = 6
SPACE = ("zh", "x", "core")
CHAN = ("zl", "y")
BF = jnp.bfloat16
F32 = jnp.float32
VMEM_LIMIT = 56 * 1024 * 1024
VM = pl.BlockSpec(memory_space=pltpu.VMEM)
KEYS = [(0, 0), (0, 1), (0, 2), (0, 3), (1, 0), (1, 1), (1, 2), (1, 3)]


def swap(v, axis, bits):
    return lax.ppermute(v, axis, [(i, i ^ bits) for i in range(lax.axis_size(axis))])


def outer_swap(v):
    pairs = []
    for i in range(1, 16, 2):
        j = (i + 1) % 16
        pairs += [(i, j), (j, i)]
    return lax.ppermute(v, SPACE, pairs)


def after(v, *deps):
    return lax.optimization_barrier((v,) + deps)[0]


def group(key):
    return (lax.axis_index("zl") ^ key[0]) * 4 + (lax.axis_index("y") ^ key[1])


def first_row(key):
    return pl.multiple_of(group(key) * 16, 16)


def lane_y():
    return lax.broadcasted_iota(jnp.int32, (16, CELLS), 1) % NXY


def from_y_before(v, y):
    return jnp.where(y == 0, pltpu.roll(v, CELLS - (NXY - 1), 1), pltpu.roll(v, 1, 1))


def from_y_after(v, y):
    return jnp.where(y == NXY - 1, pltpu.roll(v, NXY - 1, 1), pltpu.roll(v, CELLS - 1, 1))


def assemble(blocks, field, absolute, pair):
    for n, (key, (ref, start)) in enumerate(zip(KEYS, blocks)):
        row = first_row(key) if absolute else n * 16
        for z in (2 * pair, 2 * pair + 1):
            field[z, pl.ds(row, 16), :] = ref[start + z]


def pack_body(k_ref, a_ref, g_ref, by1, by3, byz, own, turned):
    turned[:, 0:432] = jnp.transpose(k_ref[...].astype(F32))
    turned[:, 432:512] = jnp.zeros((C, 80), F32)

    def piece(key):
        return turned[pl.ds(first_row(key), 16), :].astype(BF)

    own[...] = piece((0, 0))
    for dst, pairs in (
        (by1, (((0, 1), (0, 2)), ((1, 2), (1, 2)))),
        (by3, (((0, 3), (1, 3)),)),
        (byz, (((1, 0), (1, 1)),)),
    ):
        dst[pl.ds(0, N)] = a_ref[...]
        dst[pl.ds(N + len(pairs), N)] = g_ref[...]
        for n, (left, right) in enumerate(pairs):
            dst[N + n, :, 0:512] = piece(left)
            dst[N + n, :, 512:1024] = piece(right)


def unpack_filter(own, units, w_ref):
    lane = lax.broadcasted_iota(jnp.int32, (16, C), 1) // 16
    right = ((0, 2), (1, 3), (1, 1))
    pieces = [own[...].astype(F32)]
    for key, unit in zip(KEYS[1:], units[1:]):
        at = 512 if key in right else 0
        pieces.append(unit[N + 1 if key == (1, 2) else N, :, pl.ds(at, 512)].astype(F32))
    for tap in range(27):
        tile, spot = divmod(tap * 16, C)
        row = None
        for n, piece in enumerate(pieces):
            v = piece[:, tile * C : (tile + 1) * C]
            move = (n * 16 - spot) % C
            v = v if move == 0 else pltpu.roll(v, move, 1)
            row = v if row is None else jnp.where(lane == n, v, row)
        w_ref[pl.ds((26 - tap) * 16, 16), :] = row.astype(BF)


def gk_body(*refs):
    units, (g, g_in, g_out), (out,), (field, g9) = refs[:8], refs[8:11], refs[11:12], refs[12:]
    core = lax.axis_index("core")
    y = lane_y()
    for p in range(N + 2):
        if p == 0:
            plane = jnp.where(core == 0, g_out[0].astype(F32), g_in[0].astype(F32))
        elif p == N + 1:
            plane = jnp.where(core == 0, g_in[0].astype(F32), g_out[0].astype(F32))
        else:
            plane = g[p - 1].astype(F32)
        slot = N + 1 - p
        for c, v in enumerate((from_y_after(plane, y), plane, from_y_before(plane, y))):
            for b, w in enumerate((pltpu.roll(v, CELLS - NXY, 1), v, pltpu.roll(v, NXY, 1))):
                g9[pl.ds(slot * 144 + (b * 3 + c) * 16, 16), :] = w.astype(BF)
    for pair in range(N // 2):
        assemble([(u, 0) for u in units], field, True, pair)
        z = 2 * pair
        lhs = g9[pl.ds((N - 2 - z) * 144, 576), :]
        rhs = field[pl.ds(z, 2)].reshape(2 * C, CELLS)
        term = lax.dot_general(lhs, rhs, (((1,), (1,)), ((), ())), preferred_element_type=F32)
        term = term[144:576, 0:C] + term[0:432, C : 2 * C]
        if pair == 0:
            out[...] = term
        else:
            out[...] += term


def fold(t, y):
    s = t[48:96] + pltpu.roll(t[0:48], NXY, 1) + pltpu.roll(t[96:144], CELLS - NXY, 1)
    return s[16:32] + from_y_before(s[0:16], y) + from_y_after(s[32:48], y)


G_STARTS = {(0, 0): 0, (1, 2): 0, (0, 1): N + 2, (0, 2): N + 2}


def g_blocks(units):
    return [(u, G_STARTS.get(key, N + 1)) for key, u in zip(KEYS, units)]


def edges_body(*refs):
    units, (g, z2g, w, own), (inner, outer, w_in), (field,) = refs[:8], refs[8:12], refs[12:15], refs[15:]
    unpack_filter(own, units, w_in)
    y = lane_y()
    first = lax.axis_index("core") == 0
    g_units = [g, *units[1:6], z2g, units[7]]
    for n, (blocks, weights) in enumerate((([(u, 0) for u in units], w), (g_blocks(g_units), w_in))):
        for i, (key, (ref, start)) in enumerate(zip(KEYS, blocks)):
            row = first_row(key) if n == 0 else i * 16
            for k, z in enumerate((0, N - 1)):
                field[2 * n + k, pl.ds(row, 16), :] = ref[start + z]
        before = fold(jnp.dot(weights[pl.ds(288, 144), :], field[2 * n], preferred_element_type=F32), y)
        behind = fold(jnp.dot(weights[pl.ds(0, 144), :], field[2 * n + 1], preferred_element_type=F32), y)
        inner[n] = jnp.where(first, behind, before)
        outer[n] = jnp.where(first, before, behind)


def conv_body(which, *refs):
    units, w = refs[:8], refs[8]
    if which == 0:
        blocks = [(u, 0) for u in units]
        out_ref, edge, field, carry = refs[9:]
    else:
        blocks = g_blocks(units)
        inner, outer, done, edge, out_ref, done_ref, field, carry = refs[9:]
        first = lax.axis_index("core") == 0
        low = [jnp.where(first, outer[n], inner[n]) for n in range(2)]
        high = [jnp.where(first, inner[n], outer[n]) for n in range(2)]
        done_ref[0] = (edge[0] + low[0]).astype(BF)
        done_ref[pl.ds(1, N - 2)] = done[...]
        done_ref[N - 1] = (edge[1] + high[0]).astype(BF)
    y = lane_y()
    w0, w1, w2 = (w[pl.ds(a * 144, 144), :] for a in range(3))
    none = jnp.zeros((144, C), BF)
    rows = [jnp.concatenate(row, axis=1) for row in ((w2, none), (w1, w2), (w0, w1), (none, w0))]
    last = N // 2 - 1
    for pair in range(N // 2):
        assemble(blocks, field, which == 0, pair)
        rhs = field[pl.ds(2 * pair, 2)].reshape(2 * C, CELLS)
        used = range(1 if pair == 0 else 0, 3 if pair == last else 4)
        terms = jnp.dot(jnp.concatenate([rows[n] for n in used], axis=0), rhs, preferred_element_type=F32)
        for i, n in enumerate(used):
            z = 2 * pair - 1 + n
            t = terms[i * 144 : i * 144 + 144]
            if n < 2 and pair > 0:
                t = t + carry[pl.ds(n * 144, 144), :]
            if n >= 2 and pair < last:
                carry[pl.ds((n - 2) * 144, 144), :] = t
                continue
            out = fold(t, y)
            if which == 1:
                out = out + low[1] if z == 0 else out + high[1] if z == N - 1 else out
                out_ref[z] = out.astype(BF)
            elif z in (0, N - 1):
                edge[0 if z == 0 else 1] = out
            else:
                out_ref[z - 1] = out.astype(BF)


def call(body, name, args, outs, scratch=(), flops=0):
    return pl.pallas_call(
        body,
        out_shape=[jax.ShapeDtypeStruct(s, d) for s, d in outs],
        in_specs=[VM] * len(args),
        out_specs=[VM] * len(outs),
        scratch_shapes=list(scratch),
        compiler_params=pltpu.CompilerParams(vmem_limit_bytes=VMEM_LIMIT),
        cost_estimate=pl.CostEstimate(flops=flops, bytes_accessed=1 << 20, transcendentals=0),
        name=name,
    )(*args)


CONV_FLOPS = 2 * 432 * C * CELLS * N
FIELD = pltpu.VMEM((N, C, CELLS), BF)


def on_device(activation, cotangent, kernel):
    core = lax.axis_index("core")
    kt = jnp.swapaxes(kernel, 3, 4).reshape(432, C)
    plane = (16, CELLS)

    by1, by3, byz, own = call(
        pack_body,
        "pack_messages",
        [kt, activation, cotangent],
        [((N * 2 + 2, *plane), BF), ((N * 2 + 1, *plane), BF), ((N * 2 + 1, *plane), BF), ((16, 512), BF)],
        [pltpu.VMEM((C, 512), F32)],
    )
    k1 = swap(by1, "y", 1)
    k3 = swap(by3, "y", 3)
    z0 = swap(byz, "zl", 1)
    g_in = swap(jnp.where(core == 0, cotangent[N - 1 :], cotangent[:1]), "core", 1)
    g_out = outer_swap(jnp.where(core == 0, cotangent[:1], cotangent[N - 1 :]))
    k2 = swap(after(k1, g_out), "y", 3)
    z1 = swap(z0, "y", 1)
    z3 = swap(k3, "zl", 1)
    z2a = swap(k2[: N + 2], "zl", 1)
    z2g = swap(z1[N + 1 :], "y", 3)

    units = [k1, k2, k3, z0, z1, z2a, z3]
    terms = call(
        gk_body,
        "grad_kernel_terms",
        [after(activation, z2g), *units, cotangent, g_in, g_out],
        [((432, C), F32)],
        [FIELD, pltpu.VMEM(((N + 2) * 144, CELLS), BF)],
        CONV_FLOPS,
    )[0]
    terms = terms + swap(terms, "core", 1)
    got = swap(terms, "x", 1)
    inner, outer, w_in = call(
        edges_body,
        "edge_terms",
        [after(activation, terms), *units, cotangent, z2g, kt, own],
        [((2, *plane), F32)] * 2 + [((432, C), BF)],
        [pltpu.VMEM((4, C, CELLS), BF)],
        CONV_FLOPS // 9,
    )
    outer = outer_swap(outer)
    inner = swap(inner, "core", 1)
    terms = (after(terms, w_in) + got).astype(BF)
    got = swap(terms, "x", 3)
    middle, ends = call(
        functools.partial(conv_body, 0),
        "output_planes",
        [after(activation, terms), *units, kt],
        [((N - 2, *plane), BF), ((2, *plane), F32)],
        [FIELD, pltpu.VMEM((288, CELLS), F32)],
        CONV_FLOPS,
    )
    terms = after(terms, ends, outer).astype(F32) + got.astype(F32)
    got = swap(terms, "zh", 1)
    grad_input, output = call(
        functools.partial(conv_body, 1),
        "grad_input_planes",
        [after(cotangent, terms), *units[:5], z2g, z3, w_in, inner, outer, middle, ends],
        [((N, *plane), BF)] * 2,
        [FIELD, pltpu.VMEM((288, CELLS), F32)],
        CONV_FLOPS,
    )
    terms = (after(terms, grad_input) + got) * 98304.0**-0.5
    grad_kernel = jnp.swapaxes(terms.reshape(3, 3, 3, 16, C), 3, 4)
    return (output, grad_input, grad_kernel)


def solution(mesh):
    fine = Mesh(mesh.devices.reshape(2, 4, 2, 2, 4), SPACE + CHAN)
    field = P(SPACE, CHAN, None)
    filt = P(None, None, None, None, CHAN)
    return jax.shard_map(
        on_device,
        mesh=fine,
        in_specs=(field, field, filt),
        out_specs=(field, field, filt),
        check_vma=False,
    )
```

```python
import functools

import jax
import jax.numpy as jnp
from jax import lax
from jax.experimental import pallas as pl
from jax.experimental.pallas import tpu as pltpu
from jax.sharding import Mesh, PartitionSpec as P

NXY = 32
CELLS = NXY * NXY
C = 128
N = 6
SPACE = ("zh", "x", "core")
CHAN = ("zl", "y")
BF = jnp.bfloat16
F32 = jnp.float32
VMEM_LIMIT = 32 * 1024 * 1024
VM = pl.BlockSpec(memory_space=pltpu.VMEM)
KEYS = [(0, 0), (0, 1), (0, 2), (0, 3), (1, 0), (1, 1), (1, 2), (1, 3)]


def swap(v, axis, bits):
    return lax.ppermute(v, axis, [(i, i ^ bits) for i in range(lax.axis_size(axis))])


def outer_swap(v):
    pairs = []
    for i in range(1, 16, 2):
        j = (i + 1) % 16
        pairs += [(i, j), (j, i)]
    return lax.ppermute(v, SPACE, pairs)


def after(v, *deps):
    return lax.optimization_barrier((v,) + deps)[0]


def group(key):
    return (lax.axis_index("zl") ^ key[0]) * 4 + (lax.axis_index("y") ^ key[1])


def first_row(key):
    return pl.multiple_of(group(key) * 16, 16)


def lane_y():
    return lax.broadcasted_iota(jnp.int32, (16, CELLS), 1) % NXY


def from_y_before(v, y):
    return jnp.where(y == 0, pltpu.roll(v, CELLS - (NXY - 1), 1), pltpu.roll(v, 1, 1))


def from_y_after(v, y):
    return jnp.where(y == NXY - 1, pltpu.roll(v, NXY - 1, 1), pltpu.roll(v, CELLS - 1, 1))


def assemble(blocks, field, absolute, pair):
    for n, (key, (ref, start)) in enumerate(zip(KEYS, blocks)):
        row = first_row(key) if absolute else n * 16
        for z in (2 * pair, 2 * pair + 1):
            field[z, pl.ds(row, 16), :] = ref[start + z]


def pack_body(k_ref, a_ref, g_ref, by1, by3, byz, own, near, far, turned, k_in, a_in, g_in, sems):
    copies = [pltpu.make_async_copy(src, dst, sems.at[n]) for n, (src, dst) in enumerate(((k_ref, k_in), (a_ref, a_in), (g_ref, g_in)))]
    for copy in copies:
        copy.start()
    copies[0].wait()
    turned[:, 0:432] = jnp.transpose(k_in[...].astype(F32))
    turned[:, 432:512] = jnp.zeros((C, 80), F32)

    def piece(key):
        return turned[pl.ds(first_row(key), 16), :].astype(BF)

    own[...] = piece((0, 0))
    first = lax.axis_index("core") == 0
    copies[1].wait()
    copies[2].wait()
    near[0] = jnp.where(first, g_in[N - 1].astype(F32), g_in[0].astype(F32)).astype(BF)
    far[0] = jnp.where(first, g_in[0].astype(F32), g_in[N - 1].astype(F32)).astype(BF)
    for dst, pairs in (
        (by1, (((0, 1), (0, 2)),)),
        (by3, (((0, 3), (1, 3)),)),
        (byz, (((1, 0), (1, 1)), ((1, 2), (1, 2)))),
    ):
        dst[pl.ds(0, N)] = a_in[...]
        dst[pl.ds(N + len(pairs), N)] = g_in[...]
        for n, (left, right) in enumerate(pairs):
            dst[N + n, :, 0:512] = piece(left)
            dst[N + n, :, 512:1024] = piece(right)


def unpack_filter(own, units, w_ref):
    lane = lax.broadcasted_iota(jnp.int32, (16, C), 1) // 16
    right = ((0, 2), (1, 3), (1, 1))
    pieces = [own[...].astype(F32)]
    for key, unit in zip(KEYS[1:], units[1:]):
        at = 512 if key in right else 0
        pieces.append(unit[1 if key == (1, 2) else N, :, pl.ds(at, 512)].astype(F32))
    for tap in range(27):
        tile, spot = divmod(tap * 16, C)
        row = None
        for n, piece in enumerate(pieces):
            v = piece[:, tile * C : (tile + 1) * C]
            move = (n * 16 - spot) % C
            v = v if move == 0 else pltpu.roll(v, move, 1)
            row = v if row is None else jnp.where(lane == n, v, row)
        w_ref[pl.ds((26 - tap) * 16, 16), :] = row.astype(BF)


def shifts_body(g, g_in, g_out, g9):
    first = lax.axis_index("core") == 0
    y = lane_y()
    for p in range(N + 2):
        if p == 0:
            plane = jnp.where(first, g_out[0].astype(F32), g_in[0].astype(F32))
        elif p == N + 1:
            plane = jnp.where(first, g_in[0].astype(F32), g_out[0].astype(F32))
        else:
            plane = g[p - 1].astype(F32)
        slot = N + 1 - p
        for c, v in enumerate((from_y_after(plane, y), plane, from_y_before(plane, y))):
            for b, w in enumerate((pltpu.roll(v, CELLS - NXY, 1), v, pltpu.roll(v, NXY, 1))):
                g9[pl.ds(slot * 144 + (b * 3 + c) * 16, 16), :] = w.astype(BF)


def gk_body(*refs):
    units, g9, keep, send, out, field = refs[:8], *refs[8:]
    for pair in range(N // 2):
        assemble([(u, 0) for u in units], field, True, pair)
        z = 2 * pair
        lhs = g9[pl.ds((N - 2 - z) * 144, 576), :]
        rhs = field[pl.ds(z, 2)].reshape(2 * C, CELLS)
        term = lax.dot_general(lhs, rhs, (((1,), (1,)), ((), ())), preferred_element_type=F32)
        term = term[144:576, 0:C] + term[0:432, C : 2 * C]
        if pair == 0:
            out[...] = term
        else:
            out[...] += term
    core = lax.axis_index("core")
    keep[...] = out[pl.ds(pl.multiple_of(core * 216, 8), 216), :]
    send[...] = out[pl.ds(pl.multiple_of((1 - core) * 216, 8), 216), :]


def join_body(mine, other, out):
    core = lax.axis_index("core")
    scale = 98304.0**-0.5
    out[pl.ds(pl.multiple_of(core * 216, 8), 216), :] = mine[...] * scale
    out[pl.ds(pl.multiple_of((1 - core) * 216, 8), 216), :] = other[...] * scale


def fold(t, y):
    s = t[48:96] + pltpu.roll(t[0:48], NXY, 1) + pltpu.roll(t[96:144], CELLS - NXY, 1)
    return s[16:32] + from_y_before(s[0:16], y) + from_y_after(s[32:48], y)


G_STARTS = {(0, 0): 0, (1, 2): 2, (1, 0): N + 2, (1, 1): N + 2}


def g_blocks(units):
    return [(u, G_STARTS.get(key, N + 1)) for key, u in zip(KEYS, units)]


def edges_body(*refs):
    units, (g, z2g, w, own), (inner, outer, w_in), (field,) = refs[:8], refs[8:12], refs[12:15], refs[15:]
    y = lane_y()
    first = lax.axis_index("core") == 0
    g_units = [g, *units[1:6], z2g, units[7]]
    unpack_filter(own, g_units, w_in)
    for n, (blocks, weights) in enumerate((([(u, 0) for u in units], w), (g_blocks(g_units), w_in))):
        for i, (key, (ref, start)) in enumerate(zip(KEYS, blocks)):
            row = first_row(key) if n == 0 else i * 16
            for k, z in enumerate((0, N - 1)):
                field[2 * n + k, pl.ds(row, 16), :] = ref[start + z]
        before = fold(jnp.dot(weights[pl.ds(288, 144), :], field[2 * n], preferred_element_type=F32), y)
        behind = fold(jnp.dot(weights[pl.ds(0, 144), :], field[2 * n + 1], preferred_element_type=F32), y)
        inner[n] = jnp.where(first, behind, before)
        outer[n] = jnp.where(first, before, behind)


def conv_body(which, *refs):
    units, w = refs[:8], refs[8]
    if which == 0:
        blocks = [(u, 0) for u in units]
        out_ref, edge, field, carry = refs[9:]
    else:
        blocks = g_blocks(units)
        inner, outer, done, edge, out_ref, done_ref, field, carry = refs[9:]
        first = lax.axis_index("core") == 0
        low = [jnp.where(first, outer[n], inner[n]) for n in range(2)]
        high = [jnp.where(first, inner[n], outer[n]) for n in range(2)]
        done_ref[0] = (edge[0] + low[0]).astype(BF)
        done_ref[pl.ds(1, N - 2)] = done[...]
        done_ref[N - 1] = (edge[1] + high[0]).astype(BF)
    y = lane_y()
    w0, w1, w2 = (w[pl.ds(a * 144, 144), :] for a in range(3))
    none = jnp.zeros((144, C), BF)
    rows = [jnp.concatenate(row, axis=1) for row in ((w2, none), (w1, w2), (w0, w1), (none, w0))]
    last = N // 2 - 1
    for pair in range(N // 2):
        assemble(blocks, field, which == 0, pair)
        rhs = field[pl.ds(2 * pair, 2)].reshape(2 * C, CELLS)
        used = range(1 if pair == 0 else 0, 3 if pair == last else 4)
        terms = jnp.dot(jnp.concatenate([rows[n] for n in used], axis=0), rhs, preferred_element_type=F32)
        for i, n in enumerate(used):
            z = 2 * pair - 1 + n
            t = terms[i * 144 : i * 144 + 144]
            if n < 2 and pair > 0:
                t = t + carry[pl.ds(n * 144, 144), :]
            if n >= 2 and pair < last:
                carry[pl.ds((n - 2) * 144, 144), :] = t
                continue
            out = fold(t, y)
            if which == 1:
                out = out + low[1] if z == 0 else out + high[1] if z == N - 1 else out
                out_ref[z] = out.astype(BF)
            elif z in (0, N - 1):
                edge[0 if z == 0 else 1] = out
            else:
                out_ref[z - 1] = out.astype(BF)


def call(body, name, args, outs, scratch=(), flops=0, anywhere=0):
    return pl.pallas_call(
        body,
        out_shape=[jax.ShapeDtypeStruct(s, d) for s, d in outs],
        in_specs=[pl.BlockSpec(memory_space=pl.ANY)] * anywhere + [VM] * (len(args) - anywhere),
        out_specs=[VM] * len(outs),
        scratch_shapes=list(scratch),
        compiler_params=pltpu.CompilerParams(vmem_limit_bytes=VMEM_LIMIT),
        cost_estimate=pl.CostEstimate(flops=flops, bytes_accessed=1 << 20, transcendentals=0),
        name=name,
    )(*args)


CONV_FLOPS = 2 * 432 * C * CELLS * N
FIELD = pltpu.VMEM((N, C, CELLS), BF)


def on_device(activation, cotangent, kernel):
    core = lax.axis_index("core")
    kt = jnp.swapaxes(kernel, 3, 4).reshape(432, C)
    plane = (16, CELLS)

    by1, by3, byz, own, g_in, g_out = call(
        pack_body,
        "pack_messages",
        [kt, activation, cotangent],
        [((N * 2 + 1, *plane), BF), ((N * 2 + 1, *plane), BF), ((N * 2 + 2, *plane), BF), ((16, 512), BF)]
        + [((1, *plane), BF)] * 2,
        [pltpu.VMEM((C, 512), F32), pltpu.VMEM((432, C), BF)]
        + [pltpu.VMEM((N, *plane), BF)] * 2
        + [pltpu.SemaphoreType.DMA((3,))],
        anywhere=3,
    )
    k1 = swap(by1, "y", 1)
    k3 = swap(by3, "y", 3)
    z0 = swap(byz, "zl", 1)
    g_in = swap(g_in, "core", 1)
    g_out = outer_swap(g_out)
    k2 = swap(after(k1, g_out, g_in), "y", 3)
    z1 = swap(z0, "y", 1)
    z3 = swap(k3, "zl", 1)
    (moved,) = call(
        shifts_body,
        "moved_cotangent",
        [after(cotangent, k1), g_in, g_out],
        [(((N + 2) * 144, CELLS), BF)],
    )
    z2a = swap(after(k2[:N], moved), "zl", 1)
    z2g = swap(z1[N:], "y", 3)

    units = [k1, k2, k3, z0, z1, z2a, z3]
    keep, send = call(
        gk_body,
        "grad_kernel_terms",
        [activation, *units, moved],
        [((216, C), F32)] * 2,
        [pltpu.VMEM((432, C), F32), FIELD],
        CONV_FLOPS,
    )
    terms = after(keep, z2g) + swap(send, "core", 1)
    got = swap(terms, "x", 1)
    inner, outer, w_in = call(
        edges_body,
        "edge_terms",
        [after(activation, keep), *units, cotangent, z2g, kt, own],
        [((2, *plane), F32)] * 2 + [((432, C), BF)],
        [pltpu.VMEM((4, C, CELLS), BF)],
        CONV_FLOPS // 9,
    )
    outer = outer_swap(outer)
    inner = swap(inner, "core", 1)
    terms = (after(terms, w_in) + got).astype(BF)
    got = swap(terms, "x", 3)
    middle, ends = call(
        functools.partial(conv_body, 0),
        "output_planes",
        [after(activation, terms), *units, kt],
        [((N - 2, *plane), BF), ((2, *plane), F32)],
        [FIELD, pltpu.VMEM((288, CELLS), F32)],
        CONV_FLOPS,
    )
    terms = after(terms, ends, outer, inner).astype(F32) + got.astype(F32)
    got = swap(terms, "zh", 1)
    grad_input, output = call(
        functools.partial(conv_body, 1),
        "grad_input_planes",
        [after(cotangent, terms), *units[:5], z2g, z3, w_in, inner, outer, middle, ends],
        [((N, *plane), BF)] * 2,
        [FIELD, pltpu.VMEM((288, CELLS), F32)],
        CONV_FLOPS,
    )
    terms = after(terms, grad_input) + got
    (joined,) = call(join_body, "join_grad_kernel", [terms, swap(terms, "core", 1)], [((432, C), F32)])
    grad_kernel = jnp.swapaxes(joined.reshape(3, 3, 3, 16, C), 3, 4)
    return (output, grad_input, grad_kernel)


def solution(mesh):
    fine = Mesh(mesh.devices.reshape(2, 4, 2, 2, 4), SPACE + CHAN)
    field = P(SPACE, CHAN, None)
    filt = P(None, None, None, None, CHAN)
    return jax.shard_map(
        on_device,
        mesh=fine,
        in_specs=(field, field, filt),
        out_specs=(field, field, filt),
        check_vma=False,
    )
```

```python
import functools

import jax
import jax.numpy as jnp
from jax import lax
from jax.experimental import pallas as pl
from jax.experimental.pallas import tpu as pltpu
from jax.sharding import Mesh, PartitionSpec as P

NXY = 32
CELLS = NXY * NXY
C = 128
N = 6
SPACE = ("zh", "x", "core")
CHAN = ("zl", "y")
BF = jnp.bfloat16
F32 = jnp.float32
VM = pl.BlockSpec(memory_space=pltpu.VMEM)
KEYS = [(0, 0), (0, 1), (0, 2), (0, 3), (1, 0), (1, 1), (1, 2), (1, 3)]


def swap(v, axis, bits):
    return lax.ppermute(v, axis, [(i, i ^ bits) for i in range(lax.axis_size(axis))])


def outer_swap(v):
    pairs = []
    for i in range(1, 16, 2):
        j = (i + 1) % 16
        pairs += [(i, j), (j, i)]
    return lax.ppermute(v, SPACE, pairs)


def after(v, *deps):
    return lax.optimization_barrier((v,) + deps)[0]


def group(key):
    return (lax.axis_index("zl") ^ key[0]) * 4 + (lax.axis_index("y") ^ key[1])


def first_row(key):
    return pl.multiple_of(group(key) * 16, 16)


def lane_y():
    return lax.broadcasted_iota(jnp.int32, (16, CELLS), 1) % NXY


def from_y_before(v, y):
    return jnp.where(y == 0, pltpu.roll(v, CELLS - (NXY - 1), 1), pltpu.roll(v, 1, 1))


def from_y_after(v, y):
    return jnp.where(y == NXY - 1, pltpu.roll(v, NXY - 1, 1), pltpu.roll(v, CELLS - 1, 1))


def assemble(blocks, field, absolute, pair):
    for n, (key, (ref, start)) in enumerate(zip(KEYS, blocks)):
        row = first_row(key) if absolute else n * 16
        for z in (2 * pair, 2 * pair + 1):
            field[z, pl.ds(row, 16), :] = ref[start + z]


def pack_body(k_ref, a_ref, g_ref, by1, by3, byz, own, near, far, turned):
    turned[:, 0:432] = jnp.transpose(k_ref[...].astype(F32))
    turned[:, 432:512] = jnp.zeros((C, 80), F32)

    def piece(key):
        return turned[pl.ds(first_row(key), 16), :].astype(BF)

    own[...] = piece((0, 0))
    first = lax.axis_index("core") == 0
    near[0] = jnp.where(first, g_ref[N - 1].astype(F32), g_ref[0].astype(F32)).astype(BF)
    far[0] = jnp.where(first, g_ref[0].astype(F32), g_ref[N - 1].astype(F32)).astype(BF)
    for dst, pairs in (
        (by1, (((0, 1), (0, 2)),)),
        (by3, (((0, 3), (1, 3)),)),
        (byz, (((1, 0), (1, 1)), ((1, 2), (1, 2)))),
    ):
        dst[pl.ds(0, N)] = a_ref[...]
        dst[pl.ds(N + len(pairs), N)] = g_ref[...]
        for n, (left, right) in enumerate(pairs):
            dst[N + n, :, 0:512] = piece(left)
            dst[N + n, :, 512:1024] = piece(right)


def unpack_filter(own, units, w_ref):
    lane = lax.broadcasted_iota(jnp.int32, (16, C), 1) // 16
    right = ((0, 2), (1, 3), (1, 1))
    pieces = [own[...].astype(F32)]
    for key, unit in zip(KEYS[1:], units[1:]):
        at = 512 if key in right else 0
        pieces.append(unit[1 if key == (1, 2) else N, :, pl.ds(at, 512)].astype(F32))
    for tap in range(27):
        tile, spot = divmod(tap * 16, C)
        row = None
        for n, piece in enumerate(pieces):
            v = piece[:, tile * C : (tile + 1) * C]
            move = (n * 16 - spot) % C
            v = v if move == 0 else pltpu.roll(v, move, 1)
            row = v if row is None else jnp.where(lane == n, v, row)
        w_ref[pl.ds((26 - tap) * 16, 16), :] = row.astype(BF)


def shifts_body(g, g_in, g_out, g9):
    first = lax.axis_index("core") == 0
    y = lane_y()
    for p in range(N + 2):
        if p == 0:
            plane = jnp.where(first, g_out[0].astype(F32), g_in[0].astype(F32))
        elif p == N + 1:
            plane = jnp.where(first, g_in[0].astype(F32), g_out[0].astype(F32))
        else:
            plane = g[p - 1].astype(F32)
        slot = N + 1 - p
        for c, v in enumerate((from_y_after(plane, y), plane, from_y_before(plane, y))):
            for b, w in enumerate((pltpu.roll(v, CELLS - NXY, 1), v, pltpu.roll(v, NXY, 1))):
                g9[pl.ds(slot * 144 + (b * 3 + c) * 16, 16), :] = w.astype(BF)


def gk_body(*refs):
    units, g9, keep, send, out, field = refs[:8], *refs[8:]
    for pair in range(N // 2):
        assemble([(u, 0) for u in units], field, True, pair)
        z = 2 * pair
        lhs = g9[pl.ds((N - 2 - z) * 144, 576), :]
        rhs = field[pl.ds(z, 2)].reshape(2 * C, CELLS)
        term = lax.dot_general(lhs, rhs, (((1,), (1,)), ((), ())), preferred_element_type=F32)
        term = term[144:576, 0:C] + term[0:432, C : 2 * C]
        if pair == 0:
            out[...] = term
        else:
            out[...] += term
    core = lax.axis_index("core")
    keep[...] = out[pl.ds(pl.multiple_of(core * 216, 8), 216), :]
    send[...] = out[pl.ds(pl.multiple_of((1 - core) * 216, 8), 216), :]


def join_body(mine, other, out):
    core = lax.axis_index("core")
    scale = 98304.0**-0.5
    out[pl.ds(pl.multiple_of(core * 216, 8), 216), :] = mine[...] * scale
    out[pl.ds(pl.multiple_of((1 - core) * 216, 8), 216), :] = other[...] * scale


def fold(t, y):
    s = t[48:96] + pltpu.roll(t[0:48], NXY, 1) + pltpu.roll(t[96:144], CELLS - NXY, 1)
    return s[16:32] + from_y_before(s[0:16], y) + from_y_after(s[32:48], y)


G_STARTS = {(0, 0): 0, (1, 2): 2, (1, 0): N + 2, (1, 1): N + 2}


def g_blocks(units):
    return [(u, G_STARTS.get(key, N + 1)) for key, u in zip(KEYS, units)]


def edges_body(*refs):
    units, (g, z2g, w, own), (inner, outer, w_in), (field,) = refs[:8], refs[8:12], refs[12:15], refs[15:]
    y = lane_y()
    first = lax.axis_index("core") == 0
    g_units = [g, *units[1:6], z2g, units[7]]
    unpack_filter(own, g_units, w_in)
    for n, (blocks, weights) in enumerate((([(u, 0) for u in units], w), (g_blocks(g_units), w_in))):
        for i, (key, (ref, start)) in enumerate(zip(KEYS, blocks)):
            row = first_row(key) if n == 0 else i * 16
            for k, z in enumerate((0, N - 1)):
                field[2 * n + k, pl.ds(row, 16), :] = ref[start + z]
        before = fold(jnp.dot(weights[pl.ds(288, 144), :], field[2 * n], preferred_element_type=F32), y)
        behind = fold(jnp.dot(weights[pl.ds(0, 144), :], field[2 * n + 1], preferred_element_type=F32), y)
        inner[n] = jnp.where(first, behind, before)
        outer[n] = jnp.where(first, before, behind)


def conv_body(which, *refs):
    units, w = refs[:8], refs[8]
    if which == 0:
        blocks = [(u, 0) for u in units]
        out_ref, edge, field, carry = refs[9:]
    else:
        blocks = g_blocks(units)
        inner, outer, done, edge, out_ref, done_ref, field, carry = refs[9:]
        first = lax.axis_index("core") == 0
        low = [jnp.where(first, outer[n], inner[n]) for n in range(2)]
        high = [jnp.where(first, inner[n], outer[n]) for n in range(2)]
        done_ref[0] = (edge[0] + low[0]).astype(BF)
        done_ref[pl.ds(1, N - 2)] = done[...]
        done_ref[N - 1] = (edge[1] + high[0]).astype(BF)
    y = lane_y()
    w0, w1, w2 = (w[pl.ds(a * 144, 144), :] for a in range(3))
    none = jnp.zeros((144, C), BF)
    rows = [jnp.concatenate(row, axis=1) for row in ((w2, none), (w1, w2), (w0, w1), (none, w0))]
    last = N // 2 - 1
    for pair in range(N // 2):
        assemble(blocks, field, which == 0, pair)
        rhs = field[pl.ds(2 * pair, 2)].reshape(2 * C, CELLS)
        used = range(1 if pair == 0 else 0, 3 if pair == last else 4)
        terms = jnp.dot(jnp.concatenate([rows[n] for n in used], axis=0), rhs, preferred_element_type=F32)
        for i, n in enumerate(used):
            z = 2 * pair - 1 + n
            t = terms[i * 144 : i * 144 + 144]
            if n < 2 and pair > 0:
                t = t + carry[pl.ds(n * 144, 144), :]
            if n >= 2 and pair < last:
                carry[pl.ds((n - 2) * 144, 144), :] = t
                continue
            out = fold(t, y)
            if which == 1:
                out = out + low[1] if z == 0 else out + high[1] if z == N - 1 else out
                out_ref[z] = out.astype(BF)
            elif z in (0, N - 1):
                edge[0 if z == 0 else 1] = out
            else:
                out_ref[z - 1] = out.astype(BF)


def call(body, name, args, outs, scratch=(), flops=0, limit=32):
    return pl.pallas_call(
        body,
        out_shape=[jax.ShapeDtypeStruct(s, d) for s, d in outs],
        in_specs=[VM] * len(args),
        out_specs=[VM] * len(outs),
        scratch_shapes=list(scratch),
        compiler_params=pltpu.CompilerParams(vmem_limit_bytes=limit << 20),
        cost_estimate=pl.CostEstimate(flops=flops, bytes_accessed=1 << 20, transcendentals=0),
        name=name,
    )(*args)


CONV_FLOPS = 2 * 432 * C * CELLS * N
FIELD = pltpu.VMEM((N, C, CELLS), BF)


def on_device(activation, cotangent, kernel):
    core = lax.axis_index("core")
    kt = jnp.swapaxes(kernel, 3, 4).reshape(432, C)
    plane = (16, CELLS)

    by1, by3, byz, own, g_in, g_out = call(
        pack_body,
        "pack_messages",
        [kt, activation, cotangent],
        [((N * 2 + 1, *plane), BF), ((N * 2 + 1, *plane), BF), ((N * 2 + 2, *plane), BF), ((16, 512), BF)]
        + [((1, *plane), BF)] * 2,
        [pltpu.VMEM((C, 512), F32)],
        limit=56,
    )
    k1 = swap(by1, "y", 1)
    k3 = swap(by3, "y", 3)
    z0 = swap(byz, "zl", 1)
    g_in = swap(g_in, "core", 1)
    g_out = outer_swap(g_out)
    k2 = swap(after(k1, g_out, g_in), "y", 3)
    z1 = swap(z0, "y", 1)
    z3 = swap(k3, "zl", 1)
    (moved,) = call(
        shifts_body,
        "moved_cotangent",
        [after(cotangent, k1), g_in, g_out],
        [(((N + 2) * 144, CELLS), BF)],
    )
    z2a = swap(after(k2[:N], moved), "zl", 1)
    z2g = swap(z1[N:], "y", 3)

    units = [k1, k2, k3, z0, z1, z2a, z3]
    keep, send = call(
        gk_body,
        "grad_kernel_terms",
        [activation, *units, moved],
        [((216, C), F32)] * 2,
        [pltpu.VMEM((432, C), F32), FIELD],
        CONV_FLOPS,
    )
    terms = after(keep, z2g) + swap(send, "core", 1)
    got = swap(terms, "x", 1)
    inner, outer, w_in = call(
        edges_body,
        "edge_terms",
        [after(activation, keep), *units, cotangent, z2g, kt, own],
        [((2, *plane), F32)] * 2 + [((432, C), BF)],
        [pltpu.VMEM((4, C, CELLS), BF)],
        CONV_FLOPS // 9,
    )
    outer = outer_swap(outer)
    inner = swap(inner, "core", 1)
    terms = (after(terms, w_in) + got).astype(BF)
    got = swap(terms, "x", 3)
    middle, ends = call(
        functools.partial(conv_body, 0),
        "output_planes",
        [after(activation, terms), *units, kt],
        [((N - 2, *plane), BF), ((2, *plane), F32)],
        [FIELD, pltpu.VMEM((288, CELLS), F32)],
        CONV_FLOPS,
    )
    terms = after(terms, ends, outer, inner).astype(F32) + got.astype(F32)
    got = swap(terms, "zh", 1)
    grad_input, output = call(
        functools.partial(conv_body, 1),
        "grad_input_planes",
        [after(cotangent, terms), *units[:5], z2g, z3, w_in, inner, outer, middle, ends],
        [((N, *plane), BF)] * 2,
        [FIELD, pltpu.VMEM((288, CELLS), F32)],
        CONV_FLOPS,
    )
    terms = after(terms, grad_input) + got
    (joined,) = call(join_body, "join_grad_kernel", [terms, swap(terms, "core", 1)], [((432, C), F32)])
    grad_kernel = jnp.swapaxes(joined.reshape(3, 3, 3, 16, C), 3, 4)
    return (output, grad_input, grad_kernel)


def solution(mesh):
    fine = Mesh(mesh.devices.reshape(2, 4, 2, 2, 4), SPACE + CHAN)
    field = P(SPACE, CHAN, None)
    filt = P(None, None, None, None, CHAN)
    return jax.shard_map(
        on_device,
        mesh=fine,
        in_specs=(field, field, filt),
        out_specs=(field, field, filt),
        check_vma=False,
    )
```

```python
import functools

import jax
import jax.numpy as jnp
from jax import lax
from jax.experimental import pallas as pl
from jax.experimental.pallas import tpu as pltpu
from jax.sharding import Mesh, PartitionSpec as P

NXY = 32
CELLS = NXY * NXY
C = 128
N = 6
SPACE = ("zh", "x", "core")
CHAN = ("zl", "y")
BF = jnp.bfloat16
F32 = jnp.float32
VM = pl.BlockSpec(memory_space=pltpu.VMEM)
KEYS = [(0, 0), (0, 1), (0, 2), (0, 3), (1, 0), (1, 1), (1, 2), (1, 3)]


def swap(v, axis, bits):
    return lax.ppermute(v, axis, [(i, i ^ bits) for i in range(lax.axis_size(axis))])


def outer_swap(v):
    pairs = []
    for i in range(1, 16, 2):
        j = (i + 1) % 16
        pairs += [(i, j), (j, i)]
    return lax.ppermute(v, SPACE, pairs)


def after(v, *deps):
    return lax.optimization_barrier((v,) + deps)[0]


def group(key):
    return (lax.axis_index("zl") ^ key[0]) * 4 + (lax.axis_index("y") ^ key[1])


def first_row(key):
    return pl.multiple_of(group(key) * 16, 16)


def lane_y():
    return lax.broadcasted_iota(jnp.int32, (16, CELLS), 1) % NXY


def from_y_before(v, y):
    return jnp.where(y == 0, pltpu.roll(v, CELLS - (NXY - 1), 1), pltpu.roll(v, 1, 1))


def from_y_after(v, y):
    return jnp.where(y == NXY - 1, pltpu.roll(v, NXY - 1, 1), pltpu.roll(v, CELLS - 1, 1))


def assemble(blocks, field, absolute, pair):
    for n, (key, (ref, start)) in enumerate(zip(KEYS, blocks)):
        row = first_row(key) if absolute else n * 16
        for z in (2 * pair, 2 * pair + 1):
            field[z, pl.ds(row, 16), :] = ref[start + z]


def pack_body(k_ref, a_ref, g_ref, by1, by3, byz, own, near, far, turned):
    turned[:, 0:432] = jnp.transpose(k_ref[...].astype(F32))
    turned[:, 432:512] = jnp.zeros((C, 80), F32)

    def piece(key):
        return turned[pl.ds(first_row(key), 16), :].astype(BF)

    own[...] = piece((0, 0))
    first = lax.axis_index("core") == 0
    near[0] = jnp.where(first, g_ref[N - 1].astype(F32), g_ref[0].astype(F32)).astype(BF)
    far[0] = jnp.where(first, g_ref[0].astype(F32), g_ref[N - 1].astype(F32)).astype(BF)
    for dst, pairs in (
        (by1, (((0, 1), (0, 2)),)),
        (by3, (((0, 3), (1, 3)),)),
        (byz, (((1, 0), (1, 1)), ((1, 2), (1, 2)))),
    ):
        dst[pl.ds(0, N)] = a_ref[...]
        dst[pl.ds(N + len(pairs), N)] = g_ref[...]
        for n, (left, right) in enumerate(pairs):
            dst[N + n, :, 0:512] = piece(left)
            dst[N + n, :, 512:1024] = piece(right)


def unpack_filter(own, units, w_ref):
    lane = lax.broadcasted_iota(jnp.int32, (16, C), 1) // 16
    right = ((0, 2), (1, 3), (1, 1))
    pieces = [own[...].astype(F32)]
    for key, unit in zip(KEYS[1:], units[1:]):
        at = 512 if key in right else 0
        pieces.append(unit[0 if key == (1, 2) else N, :, pl.ds(at, 512)].astype(F32))
    for tap in range(27):
        tile, spot = divmod(tap * 16, C)
        row = None
        for n, piece in enumerate(pieces):
            v = piece[:, tile * C : (tile + 1) * C]
            move = (n * 16 - spot) % C
            v = v if move == 0 else pltpu.roll(v, move, 1)
            row = v if row is None else jnp.where(lane == n, v, row)
        w_ref[pl.ds((26 - tap) * 16, 16), :] = row.astype(BF)


def shifts_body(g, g_in, g_out, g9):
    first = lax.axis_index("core") == 0
    y = lane_y()
    for p in range(N + 2):
        if p == 0:
            plane = jnp.where(first, g_out[0].astype(F32), g_in[0].astype(F32))
        elif p == N + 1:
            plane = jnp.where(first, g_in[0].astype(F32), g_out[0].astype(F32))
        else:
            plane = g[p - 1].astype(F32)
        slot = N + 1 - p
        for c, v in enumerate((from_y_after(plane, y), plane, from_y_before(plane, y))):
            for b, w in enumerate((pltpu.roll(v, CELLS - NXY, 1), v, pltpu.roll(v, NXY, 1))):
                g9[pl.ds(slot * 144 + (b * 3 + c) * 16, 16), :] = w.astype(BF)


def gk_body(*refs):
    units, g9, keep, send, out, field = refs[:8], *refs[8:]
    for pair in range(N // 2):
        assemble([(u, 0) for u in units], field, True, pair)
        z = 2 * pair
        lhs = g9[pl.ds((N - 2 - z) * 144, 576), :]
        rhs = field[pl.ds(z, 2)].reshape(2 * C, CELLS)
        term = lax.dot_general(lhs, rhs, (((1,), (1,)), ((), ())), preferred_element_type=F32)
        term = term[144:576, 0:C] + term[0:432, C : 2 * C]
        if pair == 0:
            out[...] = term
        else:
            out[...] += term
    core = lax.axis_index("core")
    keep[...] = out[pl.ds(pl.multiple_of(core * 216, 8), 216), :]
    send[...] = out[pl.ds(pl.multiple_of((1 - core) * 216, 8), 216), :]


def join_body(mine, other, out):
    core = lax.axis_index("core")
    scale = 98304.0**-0.5
    out[pl.ds(pl.multiple_of(core * 216, 8), 216), :] = mine[...] * scale
    out[pl.ds(pl.multiple_of((1 - core) * 216, 8), 216), :] = other[...] * scale


def fold(t, y):
    s = t[48:96] + pltpu.roll(t[0:48], NXY, 1) + pltpu.roll(t[96:144], CELLS - NXY, 1)
    return s[16:32] + from_y_before(s[0:16], y) + from_y_after(s[32:48], y)


G_STARTS = {(0, 0): 0, (0, 2): 0, (1, 3): 0, (1, 2): 1, (1, 0): N + 2, (1, 1): N + 2}


def g_blocks(units):
    return [(u, G_STARTS.get(key, N + 1)) for key, u in zip(KEYS, units)]


def edges_body(*refs):
    units, g_units, (w, own, inner, outer, w_in, field) = refs[:8], refs[8:16], refs[16:]
    y = lane_y()
    first = lax.axis_index("core") == 0
    unpack_filter(own, [*units[:6], g_units[6], units[7]], w_in)
    for n, (blocks, weights) in enumerate((([(u, 0) for u in units], w), (g_blocks(g_units), w_in))):
        for i, (key, (ref, start)) in enumerate(zip(KEYS, blocks)):
            row = first_row(key) if n == 0 else i * 16
            for k, z in enumerate((0, N - 1)):
                field[2 * n + k, pl.ds(row, 16), :] = ref[start + z]
        before = fold(jnp.dot(weights[pl.ds(288, 144), :], field[2 * n], preferred_element_type=F32), y)
        behind = fold(jnp.dot(weights[pl.ds(0, 144), :], field[2 * n + 1], preferred_element_type=F32), y)
        inner[n] = jnp.where(first, behind, before)
        outer[n] = jnp.where(first, before, behind)


def conv_body(which, *refs):
    units, w = refs[:8], refs[8]
    if which == 0:
        blocks = [(u, 0) for u in units]
        out_ref, edge, field, carry = refs[9:]
    else:
        blocks = g_blocks(units)
        inner, outer, done, edge, out_ref, done_ref, field, carry = refs[9:]
        first = lax.axis_index("core") == 0
        low = [jnp.where(first, outer[n], inner[n]) for n in range(2)]
        high = [jnp.where(first, inner[n], outer[n]) for n in range(2)]
        done_ref[0] = (edge[0] + low[0]).astype(BF)
        done_ref[pl.ds(1, N - 2)] = done[...]
        done_ref[N - 1] = (edge[1] + high[0]).astype(BF)
    y = lane_y()
    w0, w1, w2 = (w[pl.ds(a * 144, 144), :] for a in range(3))
    none = jnp.zeros((144, C), BF)
    rows = [jnp.concatenate(row, axis=1) for row in ((w2, none), (w1, w2), (w0, w1), (none, w0))]
    last = N // 2 - 1
    for pair in range(N // 2):
        assemble(blocks, field, which == 0, pair)
        rhs = field[pl.ds(2 * pair, 2)].reshape(2 * C, CELLS)
        used = range(1 if pair == 0 else 0, 3 if pair == last else 4)
        terms = jnp.dot(jnp.concatenate([rows[n] for n in used], axis=0), rhs, preferred_element_type=F32)
        for i, n in enumerate(used):
            z = 2 * pair - 1 + n
            t = terms[i * 144 : i * 144 + 144]
            if n < 2 and pair > 0:
                t = t + carry[pl.ds(n * 144, 144), :]
            if n >= 2 and pair < last:
                carry[pl.ds((n - 2) * 144, 144), :] = t
                continue
            out = fold(t, y)
            if which == 1:
                out = out + low[1] if z == 0 else out + high[1] if z == N - 1 else out
                out_ref[z] = out.astype(BF)
            elif z in (0, N - 1):
                edge[0 if z == 0 else 1] = out
            else:
                out_ref[z - 1] = out.astype(BF)


def call(body, name, args, outs, scratch=(), flops=0, limit=32):
    return pl.pallas_call(
        body,
        out_shape=[jax.ShapeDtypeStruct(s, d) for s, d in outs],
        in_specs=[VM] * len(args),
        out_specs=[VM] * len(outs),
        scratch_shapes=list(scratch),
        compiler_params=pltpu.CompilerParams(vmem_limit_bytes=limit << 20),
        cost_estimate=pl.CostEstimate(flops=flops, bytes_accessed=1 << 20, transcendentals=0),
        name=name,
    )(*args)


CONV_FLOPS = 2 * 432 * C * CELLS * N
FIELD = pltpu.VMEM((N, C, CELLS), BF)


def on_device(activation, cotangent, kernel):
    core = lax.axis_index("core")
    kt = jnp.swapaxes(kernel, 3, 4).reshape(432, C)
    plane = (16, CELLS)

    by1, by3, byz, own, g_in, g_out = call(
        pack_body,
        "pack_messages",
        [kt, activation, cotangent],
        [((N * 2 + 1, *plane), BF), ((N * 2 + 1, *plane), BF), ((N * 2 + 2, *plane), BF), ((16, 512), BF)]
        + [((1, *plane), BF)] * 2,
        [pltpu.VMEM((C, 512), F32)],
        limit=56,
    )
    k1 = swap(by1, "y", 1)
    k3 = swap(by3, "y", 3)
    z0 = swap(byz, "zl", 1)
    g_in = swap(g_in, "core", 1)
    g_out = outer_swap(g_out)
    k2a = swap(after(k1[: N + 1], g_out), "y", 3)
    z1 = swap(after(z0, g_out, g_in), "y", 1)
    z3a = swap(k3[: N + 1], "zl", 1)
    (moved,) = call(
        shifts_body,
        "moved_cotangent",
        [after(cotangent, k1, k3), g_in, g_out],
        [(((N + 2) * 144, CELLS), BF)],
    )
    z2a = swap(after(k2a[:N], moved), "zl", 1)
    g3 = after(k3[N + 1 :], k2a)
    z3g = swap(g3, "zl", 1)
    k2g = swap(g3, "y", 1)
    z2g = swap(z1[N + 1 :], "y", 3)

    units = [activation, k1, k2a, k3, z0, z1, z2a, z3a]
    g_units = [cotangent, k1, k2g, k3, z0, z1, z2g, z3g]
    keep, send = call(
        gk_body,
        "grad_kernel_terms",
        [*units, moved],
        [((216, C), F32)] * 2,
        [pltpu.VMEM((432, C), F32), FIELD],
        CONV_FLOPS,
    )
    terms = after(keep, z2g, k2g, z3g) + swap(send, "core", 1)
    got = swap(terms, "x", 1)
    inner, outer, w_in = call(
        edges_body,
        "edge_terms",
        [*units, *g_units, after(kt, keep), own],
        [((2, *plane), F32)] * 2 + [((432, C), BF)],
        [pltpu.VMEM((4, C, CELLS), BF)],
        CONV_FLOPS // 9,
    )
    outer = outer_swap(outer)
    inner = swap(inner, "core", 1)
    terms = (after(terms, w_in) + got).astype(BF)
    got = swap(terms, "x", 3)
    middle, ends = call(
        functools.partial(conv_body, 0),
        "output_planes",
        [*units, after(kt, terms)],
        [((N - 2, *plane), BF), ((2, *plane), F32)],
        [FIELD, pltpu.VMEM((288, CELLS), F32)],
        CONV_FLOPS,
    )
    terms = after(terms, ends, outer, inner).astype(F32) + got.astype(F32)
    got = swap(terms, "zh", 1)
    grad_input, output = call(
        functools.partial(conv_body, 1),
        "grad_input_planes",
        [*g_units, after(w_in, terms), inner, outer, middle, ends],
        [((N, *plane), BF)] * 2,
        [FIELD, pltpu.VMEM((288, CELLS), F32)],
        CONV_FLOPS,
    )
    terms = after(terms, grad_input) + got
    (joined,) = call(join_body, "join_grad_kernel", [terms, swap(terms, "core", 1)], [((432, C), F32)])
    grad_kernel = jnp.swapaxes(joined.reshape(3, 3, 3, 16, C), 3, 4)
    return (output, grad_input, grad_kernel)


def solution(mesh):
    fine = Mesh(mesh.devices.reshape(2, 4, 2, 2, 4), SPACE + CHAN)
    field = P(SPACE, CHAN, None)
    filt = P(None, None, None, None, CHAN)
    return jax.shard_map(
        on_device,
        mesh=fine,
        in_specs=(field, field, filt),
        out_specs=(field, field, filt),
        check_vma=False,
    )
```

```python
import functools

import jax
import jax.numpy as jnp
from jax import lax
from jax.experimental import pallas as pl
from jax.experimental.pallas import tpu as pltpu
from jax.sharding import Mesh, PartitionSpec as P

NXY = 32
CELLS = NXY * NXY
C = 128
N = 6
SPACE = ("zh", "x", "core")
CHAN = ("zl", "y")
BF = jnp.bfloat16
F32 = jnp.float32
VM = pl.BlockSpec(memory_space=pltpu.VMEM)
KEYS = [(0, 0), (0, 1), (0, 2), (0, 3), (1, 0), (1, 1), (1, 2), (1, 3)]


def swap(v, axis, bits):
    return lax.ppermute(v, axis, [(i, i ^ bits) for i in range(lax.axis_size(axis))])


def outer_swap(v):
    pairs = []
    for i in range(1, 16, 2):
        j = (i + 1) % 16
        pairs += [(i, j), (j, i)]
    return lax.ppermute(v, SPACE, pairs)


def after(v, *deps):
    return lax.optimization_barrier((v,) + deps)[0]


def group(key):
    return (lax.axis_index("zl") ^ key[0]) * 4 + (lax.axis_index("y") ^ key[1])


def first_row(key):
    return pl.multiple_of(group(key) * 16, 16)


def lane_y():
    return lax.broadcasted_iota(jnp.int32, (16, CELLS), 1) % NXY


def from_y_before(v, y):
    return jnp.where(y == 0, pltpu.roll(v, CELLS - (NXY - 1), 1), pltpu.roll(v, 1, 1))


def from_y_after(v, y):
    return jnp.where(y == NXY - 1, pltpu.roll(v, NXY - 1, 1), pltpu.roll(v, CELLS - 1, 1))


def assemble(blocks, field, absolute, pair):
    for n, (key, (ref, start)) in enumerate(zip(KEYS, blocks)):
        row = first_row(key) if absolute else n * 16
        for z in (2 * pair, 2 * pair + 1):
            field[z, pl.ds(row, 16), :] = ref[start + z]


def pack_body(k_ref, a_ref, g_ref, by1, by3, byz, own, near, far, turned):
    turned[:, 0:432] = jnp.transpose(k_ref[...].astype(F32))
    turned[:, 432:512] = jnp.zeros((C, 80), F32)

    def piece(key):
        return turned[pl.ds(first_row(key), 16), :].astype(BF)

    own[...] = piece((0, 0))
    first = lax.axis_index("core") == 0
    near[0] = jnp.where(first, g_ref[N - 1].astype(F32), g_ref[0].astype(F32)).astype(BF)
    far[0] = jnp.where(first, g_ref[0].astype(F32), g_ref[N - 1].astype(F32)).astype(BF)
    for dst, pairs in (
        (by1, (((0, 1), (0, 2)),)),
        (by3, (((0, 3), (1, 3)),)),
        (byz, (((1, 0), (1, 1)), ((1, 2), (1, 2)))),
    ):
        dst[pl.ds(0, N)] = a_ref[...]
        dst[pl.ds(N + len(pairs), N)] = g_ref[...]
        for n, (left, right) in enumerate(pairs):
            dst[N + n, :, 0:512] = piece(left)
            dst[N + n, :, 512:1024] = piece(right)


def unpack_filter(own, units, w_ref):
    lane = lax.broadcasted_iota(jnp.int32, (16, C), 1) // 16
    right = ((0, 2), (1, 3), (1, 1))
    pieces = [own[...].astype(F32)]
    for key, unit in zip(KEYS[1:], units[1:]):
        at = 512 if key in right else 0
        pieces.append(unit[0 if key == (1, 2) else N, :, pl.ds(at, 512)].astype(F32))
    for tap in range(27):
        tile, spot = divmod(tap * 16, C)
        row = None
        for n, piece in enumerate(pieces):
            v = piece[:, tile * C : (tile + 1) * C]
            move = (n * 16 - spot) % C
            v = v if move == 0 else pltpu.roll(v, move, 1)
            row = v if row is None else jnp.where(lane == n, v, row)
        w_ref[pl.ds((26 - tap) * 16, 16), :] = row.astype(BF)


def shifts_body(g, g_in, g_out, g9):
    first = lax.axis_index("core") == 0
    y = lane_y()
    for p in range(N + 2):
        if p == 0:
            plane = jnp.where(first, g_out[0].astype(F32), g_in[0].astype(F32))
        elif p == N + 1:
            plane = jnp.where(first, g_in[0].astype(F32), g_out[0].astype(F32))
        else:
            plane = g[p - 1].astype(F32)
        slot = N + 1 - p
        for c, v in enumerate((from_y_after(plane, y), plane, from_y_before(plane, y))):
            for b, w in enumerate((pltpu.roll(v, CELLS - NXY, 1), v, pltpu.roll(v, NXY, 1))):
                g9[pl.ds(slot * 144 + (b * 3 + c) * 16, 16), :] = w.astype(BF)


def gk_body(*refs):
    units, g9, keep, send, out, field = refs[:8], *refs[8:]
    for pair in range(N // 2):
        assemble([(u, 0) for u in units], field, True, pair)
        z = 2 * pair
        lhs = g9[pl.ds((N - 2 - z) * 144, 576), :]
        rhs = field[pl.ds(z, 2)].reshape(2 * C, CELLS)
        term = lax.dot_general(lhs, rhs, (((1,), (1,)), ((), ())), preferred_element_type=F32)
        term = term[144:576, 0:C] + term[0:432, C : 2 * C]
        if pair == 0:
            out[...] = term
        else:
            out[...] += term
    core = lax.axis_index("core")
    keep[...] = out[pl.ds(pl.multiple_of(core * 216, 8), 216), :]
    send[...] = out[pl.ds(pl.multiple_of((1 - core) * 216, 8), 216), :]


def join_body(mine, other, out):
    core = lax.axis_index("core")
    scale = 98304.0**-0.5
    out[pl.ds(pl.multiple_of(core * 216, 8), 216), :] = mine[...] * scale
    out[pl.ds(pl.multiple_of((1 - core) * 216, 8), 216), :] = other[...] * scale


def fold(t, y):
    s = t[48:96] + pltpu.roll(t[0:48], NXY, 1) + pltpu.roll(t[96:144], CELLS - NXY, 1)
    return s[16:32] + from_y_before(s[0:16], y) + from_y_after(s[32:48], y)


G_STARTS = {(0, 0): 0, (0, 2): 0, (1, 3): 0, (1, 2): 1, (1, 0): N + 2, (1, 1): N + 2}


def g_blocks(units):
    return [(u, G_STARTS.get(key, N + 1)) for key, u in zip(KEYS, units)]


def edges_body(*refs):
    units, g_units, (w, own, inner, outer, w_in, field) = refs[:8], refs[8:16], refs[16:]
    y = lane_y()
    first = lax.axis_index("core") == 0
    unpack_filter(own, [*units[:6], g_units[6], units[7]], w_in)
    for n, (blocks, weights) in enumerate((([(u, 0) for u in units], w), (g_blocks(g_units), w_in))):
        for i, (key, (ref, start)) in enumerate(zip(KEYS, blocks)):
            row = first_row(key) if n == 0 else i * 16
            for k, z in enumerate((0, N - 1)):
                field[2 * n + k, pl.ds(row, 16), :] = ref[start + z]
        before = fold(jnp.dot(weights[pl.ds(288, 144), :], field[2 * n], preferred_element_type=F32), y)
        behind = fold(jnp.dot(weights[pl.ds(0, 144), :], field[2 * n + 1], preferred_element_type=F32), y)
        inner[n] = jnp.where(first, behind, before)
        outer[n] = jnp.where(first, before, behind)


def conv_body(which, *refs):
    units, w = refs[:8], refs[8]
    if which == 0:
        blocks = [(u, 0) for u in units]
        out_ref, edge, field, carry = refs[9:]
    else:
        blocks = g_blocks(units)
        inner, outer, done, edge, out_ref, done_ref, field, carry = refs[9:]
        first = lax.axis_index("core") == 0
        low = [jnp.where(first, outer[n], inner[n]) for n in range(2)]
        high = [jnp.where(first, inner[n], outer[n]) for n in range(2)]
        done_ref[0] = (edge[0] + low[0]).astype(BF)
        done_ref[pl.ds(1, N - 2)] = done[...]
        done_ref[N - 1] = (edge[1] + high[0]).astype(BF)
    y = lane_y()
    w0, w1, w2 = (w[pl.ds(a * 144, 144), :] for a in range(3))
    none = jnp.zeros((144, C), BF)
    rows = [jnp.concatenate(row, axis=1) for row in ((w2, none), (w1, w2), (w0, w1), (none, w0))]
    last = N // 2 - 1
    for pair in range(N // 2):
        assemble(blocks, field, which == 0, pair)
        rhs = field[pl.ds(2 * pair, 2)].reshape(2 * C, CELLS)
        used = range(1 if pair == 0 else 0, 3 if pair == last else 4)
        terms = jnp.dot(jnp.concatenate([rows[n] for n in used], axis=0), rhs, preferred_element_type=F32)
        for i, n in enumerate(used):
            z = 2 * pair - 1 + n
            t = terms[i * 144 : i * 144 + 144]
            if n < 2 and pair > 0:
                t = t + carry[pl.ds(n * 144, 144), :]
            if n >= 2 and pair < last:
                carry[pl.ds((n - 2) * 144, 144), :] = t
                continue
            out = fold(t, y)
            if which == 1:
                out = out + low[1] if z == 0 else out + high[1] if z == N - 1 else out
                out_ref[z] = out.astype(BF)
            elif z in (0, N - 1):
                edge[0 if z == 0 else 1] = out
            else:
                out_ref[z - 1] = out.astype(BF)


def call(body, name, args, outs, scratch=(), flops=0, limit=32):
    return pl.pallas_call(
        body,
        out_shape=[jax.ShapeDtypeStruct(s, d) for s, d in outs],
        in_specs=[VM] * len(args),
        out_specs=[VM] * len(outs),
        scratch_shapes=list(scratch),
        compiler_params=pltpu.CompilerParams(vmem_limit_bytes=limit << 20),
        cost_estimate=pl.CostEstimate(flops=flops, bytes_accessed=1 << 20, transcendentals=0),
        name=name,
    )(*args)


CONV_FLOPS = 2 * 432 * C * CELLS * N
FIELD = pltpu.VMEM((N, C, CELLS), BF)


def on_device(activation, cotangent, kernel):
    core = lax.axis_index("core")
    kt = jnp.swapaxes(kernel, 3, 4).reshape(432, C)
    plane = (16, CELLS)

    by1, by3, byz, own, g_in, g_out = call(
        pack_body,
        "pack_messages",
        [kt, activation, cotangent],
        [((N * 2 + 1, *plane), BF), ((N * 2 + 1, *plane), BF), ((N * 2 + 2, *plane), BF), ((16, 512), BF)]
        + [((1, *plane), BF)] * 2,
        [pltpu.VMEM((C, 512), F32)],
        limit=56,
    )
    k1 = swap(by1, "y", 1)
    k3 = swap(by3, "y", 3)
    z0 = swap(byz, "zl", 1)
    g_in = swap(g_in, "core", 1)
    g_out = outer_swap(g_out)
    k2a = swap(after(k1[: N + 1], g_out), "y", 3)
    z1 = swap(after(z0, g_out, g_in), "y", 1)
    z3a = swap(k3[: N + 1], "zl", 1)
    (moved,) = call(
        shifts_body,
        "moved_cotangent",
        [after(cotangent, k1, k3), g_in, g_out],
        [(((N + 2) * 144, CELLS), BF)],
    )
    z2a = swap(after(k2a[:N], moved), "zl", 1)
    g3 = after(k3[N + 1 :], k2a)
    z3g = swap(g3, "zl", 1)
    k2g = swap(g3, "y", 1)
    z2g = swap(z1[N + 1 :], "y", 3)

    units = [activation, k1, k2a, k3, z0, z1, z2a, z3a]
    g_units = [cotangent, k1, k2g, k3, z0, z1, z2g, z3g]
    keep, send = call(
        gk_body,
        "grad_kernel_terms",
        [*units, moved],
        [((216, C), F32)] * 2,
        [pltpu.VMEM((432, C), F32), FIELD],
        CONV_FLOPS,
    )
    terms = after(keep, k2g, z3g) + swap(send, "core", 1)
    got = swap(terms, "x", 1)
    inner, outer, w_in = call(
        edges_body,
        "edge_terms",
        [*units, *g_units, after(kt, keep), own],
        [((2, *plane), F32)] * 2 + [((432, C), BF)],
        [pltpu.VMEM((4, C, CELLS), BF)],
        CONV_FLOPS // 9,
    )
    outer = outer_swap(outer)
    inner = swap(inner, "core", 1)
    terms = (after(terms, w_in) + got).astype(BF)
    got = swap(terms, "x", 3)
    middle, ends = call(
        functools.partial(conv_body, 0),
        "output_planes",
        [*units, after(kt, terms)],
        [((N - 2, *plane), BF), ((2, *plane), F32)],
        [FIELD, pltpu.VMEM((288, CELLS), F32)],
        CONV_FLOPS,
    )
    terms = after(terms, ends, outer, inner).astype(F32) + got.astype(F32)
    got = swap(terms, "zh", 1)
    grad_input, output = call(
        functools.partial(conv_body, 1),
        "grad_input_planes",
        [*g_units, after(w_in, terms), inner, outer, middle, ends],
        [((N, *plane), BF)] * 2,
        [FIELD, pltpu.VMEM((288, CELLS), F32)],
        CONV_FLOPS,
    )
    terms = after(terms, grad_input) + got
    (joined,) = call(join_body, "join_grad_kernel", [terms, swap(terms, "core", 1)], [((432, C), F32)])
    grad_kernel = jnp.swapaxes(joined.reshape(3, 3, 3, 16, C), 3, 4)
    return (output, grad_input, grad_kernel)


def solution(mesh):
    fine = Mesh(mesh.devices.reshape(2, 4, 2, 2, 4), SPACE + CHAN)
    field = P(SPACE, CHAN, None)
    filt = P(None, None, None, None, CHAN)
    return jax.shard_map(
        on_device,
        mesh=fine,
        in_specs=(field, field, filt),
        out_specs=(field, field, filt),
        check_vma=False,
    )
```
